128 devices in a mesh: stream: 8 (over y, core), girth: 16 (over z, x).
Axes of the slice: x: 4, y: 4, z: 4, core: 2. Of those that a mesh axis runs over, the one named last changes fastest.
Arguments:
- iterate: float32 [7, 16, 64, 256, 128], P(None, None, 'stream', 'girth'), may hold values from -6 to 6
- right_side: float32 [7, 16, 64, 256, 128], P(None, None, 'stream', 'girth'), may hold values from -6 to 6
- block_inverse: float32 [7, 7, 64, 256, 128], P(None, None, 'stream', 'girth'), may hold values from -0.6 to 1, as said below
- face_weight: float32 [6, 64, 256, 128], P(None, 'stream', 'girth'), may hold values from 0.05 to 0.5
- face_jacobian: float32 [6, 7, 7], replicated, may hold values from -2 to 2
- wall_cell: int32 [32768], P(('stream', 'girth')), may hold values from 0 to 16383
- wall_owner: int32 [32768, 1], P(('stream', 'girth')), may hold values from 0 to 127; in each aligned block of 256 rows (0 to 255, 256 to 511, ...) at most 8 rows name the same one
- wall_patch: int32 [32768], P(('stream', 'girth')), may hold values from 0 to 31
- wall_shape: float32 [32768, 8], P(('stream', 'girth')), may hold values from -20 to 20
Outputs:
- updated: float32 [7, 16, 64, 256, 128], P(None, None, 'stream', 'girth')
- patch_force: float32 [4096, 128], P(('stream', 'girth'))
- force: float32 [8, 16], replicated
The draws below stay inside these ranges and needn't reach their ends.
Inputs may be any that keep to these rules, and one draw needn't show every extreme that they name: `block_inverse`: diagonal entries lie in 0.3 to 1, the others lie in -0.6 to 0.6. `wall_owner`: of the rows of one device at most 8 name one owner.
All inputs are finite; a program needn't handle non-finite values.
Results may differ from the reference program's by a relative error of at most 0.0001.
Values sent between devices are 32-bit elements; how exact they have to be, the bound alone decides.
A program may use at most 192 MiB of HBM per device.

```python
import math
import jax
import jax.numpy as jnp
import numpy as np
from jax import lax

VARS = 7
MODES = 8
RHS = 16
CX = 8
CG = 16
NR = 128
WALL_DEV = 256
PATCH_DEV = 32
NX = 64
NG = 256
WALLS = 32768
PATCHES = 4096
CAP = 8
N_STREAM = 8
N_GIRTH = 16


def draw_block_inverse(key, part):
    key = jax.random.fold_in(key, 11)
    shape = (VARS, VARS, NX, NG, NR)
    first, second = jax.random.split(key)
    row = lax.broadcasted_iota(jnp.int32, shape, 0)
    column = lax.broadcasted_iota(jnp.int32, shape, 1)
    main = jnp.exp(jax.random.uniform(first, shape, jnp.float32, jnp.log(0.3), 0.0))
    side = jnp.clip(0.12 * jax.random.normal(second, shape, jnp.float32), -0.6, 0.6)
    return jnp.where(row == column, main, side).astype(jnp.float32)


def draw_wall_shape(key, part):
    key = jax.random.fold_in(key, 23)
    shape = (WALLS, MODES)
    first = jax.random.fold_in(key, 0)
    device = lax.broadcasted_iota(jnp.int32, shape, 0) // WALL_DEV
    rise = 1.0 + 2.0 * device.astype(jnp.float32) / jnp.float32(WALLS // WALL_DEV - 1)
    values = jnp.clip(jax.random.normal(first, shape, jnp.float32), -4.0, 4.0) * rise
    return values.astype(jnp.float32)


def plant(array, key, low, largest):
    longest = array.shape.index(max(array.shape))
    spots = []
    for shift in (0, 1):
        where = [jax.random.randint(jax.random.fold_in(key, axis), (), 0, length) for axis, length in enumerate(array.shape)]
        where[longest] = (where[longest] + shift) % array.shape[longest]
        spots.append(tuple(where))
    return array.at[spots[0]].set(low).at[spots[1]].set(largest)


def steps_of(own_key, shape, cuts, low, largest):
    level = 1.0
    for position, shards_of in cuts:
        draws = jax.random.uniform(jax.random.fold_in(jax.random.fold_in(own_key, 6), position), (shards_of,), jnp.float32, low / len(cuts), largest / len(cuts))
        level = level * jnp.repeat(jnp.exp(draws), shape[position] // shards_of).reshape((-1,) + (1,) * (len(shape) - 1 - position))
    return level


def assign_block(stream_key, own, number, rows, count, top, bound, skew):
    ranking = jax.random.permutation(stream_key, count)
    crowded, common = load_shares(count, rows * top, bound, skew, True), load_shares(count, rows * top, bound, skew, False)
    places = jnp.arange(count)

    def named(lengths, offset_by):
        used = int((lengths > 0).sum())
        fixed = max(1, used // 4)
        shifted = fixed + (places - fixed + offset_by * (used - fixed)) % max(1, count - fixed)
        return jnp.zeros((count,), jnp.int32).at[ranking[jnp.where(places < fixed, places, shifted)]].set(jnp.asarray(lengths, jnp.int32))

    lengths = jnp.where(number % 4 == 0, named(crowded, number // 4), named(common, number - number // 4 - 1))
    mixed = jax.random.permutation(jax.random.fold_in(own, 3), count)
    source_of, sink = mixed[0:count // 2 * 2:2], mixed[1:count // 2 * 2:2]
    room = jnp.minimum(lengths[source_of] - 1, bound - lengths[sink]) // 2
    room = jnp.where((source_of == ranking[0]) | (sink == ranking[0]) | (lengths[sink] == 0), 0, jnp.maximum(room, 0))
    shifted = jax.random.randint(jax.random.fold_in(own, 4), (count // 2,), 0, 1 << 20) % (room + 1)
    lengths = lengths.at[source_of].add(-shifted).at[sink].add(shifted)
    members = jnp.searchsorted(jnp.cumsum(lengths), jnp.arange(rows * top), side="right").astype(jnp.int32)
    table = members.reshape(top, rows).T
    table = table[jax.random.permutation(jax.random.fold_in(own, 1), rows)]
    offset_by = jax.random.randint(jax.random.fold_in(own, 2), (rows, 1), 0, top)
    return jnp.take_along_axis(table, (jnp.arange(top)[None, :] + offset_by) % top, axis=1)


def load_shares(amount, total, limit, slope, full):
    loads = [(1 << 20) // math.isqrt(rank ** slope) + 1 for rank in range(1, amount + 1)]
    largest = limit if full else min(limit, max(-(-total // amount), total * loads[0] // sum(loads)))
    least = 1 if total - largest >= amount - 1 else 0
    given, spare = [largest] + [least] * (amount - 1), total - largest - least * (amount - 1)
    while spare > 0:
        candidates = [i for i in range(1, amount) if given[i] < largest] or [i for i in range(1, amount) if given[i] < limit]
        pool, budget = sum([loads[i] for i in candidates]), spare
        for i in candidates:
            extra = min(limit - given[i], max(1, budget * loads[i] // pool), spare)
            given[i] = given[i] + extra
            spare = spare - extra
    return np.array(given)


def scatter_about(stream_key, extent, deviation, reach, cuts=(), held_as=jnp.bfloat16):
    array = jax.random.normal(stream_key, extent, jnp.float32) * deviation
    if len(cuts) > 0:
        array = steps_of(stream_key, extent, cuts, -0.22, 0.18) * array
    return jnp.clip(array, min=-reach, max=reach).astype(held_as)


def setup_inputs(seed: int = 0) -> dict:
    splits = jax.random.split(jax.random.key(seed), 10)
    iterate = scatter_about(splits[0], (VARS, RHS, NX, NG, NR), 1.0, 6.0, ((2, 8), (3, 16)), jnp.float32)
    right_side = scatter_about(splits[1], (VARS, RHS, NX, NG, NR), 1.0, 6.0, ((2, 8), (3, 16)), jnp.float32)
    block_inverse = draw_block_inverse(jax.random.fold_in(splits[9], 71), 0)
    face_weight = jnp.clip(jnp.exp(math.log(0.5) - 2.3025851 * jax.random.uniform(splits[3], (6, NX, NG, NR), jnp.float32) ** steps_of(splits[3], (6, NX, NG, NR), ((1, 8), (2, 16)), -0.2, 0.2)), 0.05, 0.5)
    face_jacobian = scatter_about(splits[4], (6, VARS, VARS), VARS ** -0.5, 2.0, (), jnp.float32)
    wall_cell = plant(jax.random.randint(splits[5], (WALLS,), 0, CX * CG * NR), jax.random.fold_in(splits[5], 1), 0, (CX * CG * NR) - 1).astype(jnp.int32)
    wall_owner_keys = jax.random.split(jax.random.fold_in(splits[6], 1), WALLS // WALL_DEV)
    wall_owner_turns = jax.random.permutation(jax.random.fold_in(splits[6], 3), WALLS // WALL_DEV)
    wall_owner = jax.vmap(lambda own, number: assign_block(jax.random.fold_in(splits[6], 2), own, number, WALL_DEV, N_STREAM * N_GIRTH, 1, CAP, 2))(wall_owner_keys, wall_owner_turns).reshape((WALLS, 1))
    wall_patch = plant(jax.random.randint(splits[7], (WALLS,), 0, PATCH_DEV), jax.random.fold_in(splits[7], 1), 0, PATCH_DEV - 1).astype(jnp.int32)
    wall_shape = draw_wall_shape(jax.random.fold_in(splits[9], 71), 0)
    return {"iterate": iterate, "right_side": right_side, "block_inverse": block_inverse, "face_weight": face_weight, "face_jacobian": face_jacobian, "wall_cell": wall_cell, "wall_owner": wall_owner, "wall_patch": wall_patch, "wall_shape": wall_shape}


def apply_jacobian(jacobian, field):
    return jnp.einsum('uv,vkxgr->ukxgr', jacobian, field, precision=lax.Precision.HIGHEST)

def reference(iterate, right_side, block_inverse, face_weight, face_jacobian, wall_cell, wall_owner, wall_patch, wall_shape):
    zero_pad = jnp.pad(iterate, ((0, 0), (0, 0), (1, 1), (1, 1), (1, 1)))
    pieces = [zero_pad[:, :, 0:NX, 1:NG + 1, 1:NR + 1], zero_pad[:, :, 2:NX + 2, 1:NG + 1, 1:NR + 1], zero_pad[:, :, 1:NX + 1, 0:NG, 1:NR + 1], zero_pad[:, :, 1:NX + 1, 2:NG + 2, 1:NR + 1], zero_pad[:, :, 1:NX + 1, 1:NG + 1, 0:NR], zero_pad[:, :, 1:NX + 1, 1:NG + 1, 2:NR + 2]]
    coupling = jnp.zeros(iterate.shape, jnp.float32)
    for face in range(6):
        coupling = coupling + face_weight[face][None, None] * apply_jacobian(face_jacobian[face], pieces[face])
    remainder = right_side - coupling
    updated = jnp.zeros(iterate.shape, jnp.float32)
    for column in range(VARS):
        updated = updated + block_inverse[:, column][:, None] * remainder[column][None]
    device = jnp.arange(WALLS, dtype=jnp.int32) // WALL_DEV
    stream_idx = device // N_GIRTH
    girth_idx = device % N_GIRTH
    local_x = wall_cell // (CG * NR)
    local_g = wall_cell // NR % CG
    local_r = wall_cell % NR
    global_x = stream_idx * CX + local_x
    global_g = girth_idx * CG + local_g
    pressure = updated[0][:, global_x, global_g, local_r]
    contribution = (wall_shape[:, :, None] * jnp.transpose(pressure)[:, None, :]).reshape(WALLS, MODES * RHS)
    segment = wall_owner[:, 0] * PATCH_DEV + wall_patch
    patch_force = jax.ops.segment_sum(contribution, segment, num_segments=PATCHES)
    force = (lax.optimization_barrier(jnp.sum(contribution, axis=0)) / jnp.sqrt(jnp.float32(WALLS))).reshape(MODES, RHS)
    return (updated, patch_force, force)
```

```python
import jax
import jax.numpy as jnp
from jax import lax
from jax.experimental import pallas as pl
from jax.experimental.pallas import tpu as pltpu
from jax.sharding import PartitionSpec as P

V = 7
K = 16
CX = 8
CG = 16
NR = 128
ROWS = CX * CG
SLOTS = 256
PATCH_DEV = 32
NS = 8
NG = 16
DEV = NS * NG
PAIRS = K // 2
PACK_1 = 2 * NG + 8
DEPTH = 176
BLK = V * 8
MESH = pl.DeviceIdType.MESH
HIGH = lax.Precision.HIGHEST
F32 = jnp.float32
BF16 = jnp.bfloat16
WEST, EAST, SOUTH, NORTH = range(4)


def nt(a, b, precision=None):
    return lax.dot_general(
        a, b, (((1,), (1,)), ((), ())), precision=precision, preferred_element_type=F32
    )


def split(x):
    hi = x.astype(BF16).astype(F32)
    return hi, x - hi


def operator(jacobian, turn):
    r = lax.broadcasted_iota(jnp.int32, (BLK, V), 0)
    c = lax.broadcasted_iota(jnp.int32, (BLK, V), 1)
    rows = (r // 8 == c).astype(F32)
    r = lax.broadcasted_iota(jnp.int32, (V, DEPTH), 0)
    c = lax.broadcasted_iota(jnp.int32, (V, DEPTH), 1)
    columns = ((c % BLK) // 8 == r).astype(F32)
    spread = jnp.dot(jnp.dot(rows, jacobian, precision=HIGH), columns, precision=HIGH)
    hi, lo = split(spread)
    r = lax.broadcasted_iota(jnp.int32, (BLK, DEPTH), 0)
    c = lax.broadcasted_iota(jnp.int32, (BLK, DEPTH), 1)
    keep = ((r + turn) % 8 == c % 8) & (c < 3 * BLK)
    return jnp.where(keep, jnp.where(c < 2 * BLK, hi, lo), 0.0)


def operand(load):
    x = jnp.concatenate([load(v) for v in range(V)], axis=0)
    hi, lo = split(x)
    pad = jnp.zeros((DEPTH - 3 * BLK, 2 * NR), F32)
    return jnp.concatenate([x, lo, x, pad], axis=0).astype(BF16)


def sweep_kernel(
    it, rhs, binv, fw, jac_in, cell_in, owner_in, patch_in, shape_in,
    upd, arrived_out,
    it_v, rhs_v, binv_v, fw_v, halo_x, halo_g, send_g, wmain, wside, edge, pick,
    jac, cell, owner, patch, shape, send_1, arrived_1, send_2, arrived_2,
    sem_it, sem_rhs, sem_misc, send_sem, recv_sem, send_sem_1, recv_sem_1, send_sem_2, recv_sem_2,
):
    s, g = lax.axis_index("stream"), lax.axis_index("girth")
    present = (s > 0, s < NS - 1, g > 0, g < NG - 1)
    target = ((s - 1, g), (s + 1, g), (s, g - 1), (s, g + 1))

    def it_copy(c):
        ks = pl.ds(2 * c, 2)
        return pltpu.make_async_copy(it.at[:, ks], it_v.at[:, ks], sem_it.at[c])

    def rhs_copy(c):
        ks = pl.ds(2 * c, 2)
        return pltpu.make_async_copy(rhs.at[:, ks], rhs_v.at[:, ks], sem_rhs.at[c])

    singles = [
        pltpu.make_async_copy(a, b, sem_misc.at[i])
        for i, (a, b) in enumerate(
            (
                (jac_in, jac),
                (cell_in, cell),
                (owner_in, owner),
                (patch_in, patch),
                (shape_in, shape),
                (fw, fw_v),
                (binv, binv_v),
            )
        )
    ]

    def halo_copy(side, c, land=None):
        land = side ^ 1 if land is None else land
        ks = pl.ds(2 * c, 2)
        if side in (WEST, EAST):
            rows = pl.ds(0 if side == WEST else ROWS - CG, CG)
            src, dst = it.at[:, ks, rows], halo_x.at[land, :, ks]
        else:
            src, dst = send_g.at[side - 2, :, ks], halo_g.at[land - 2, :, ks]
        return pltpu.make_async_remote_copy(
            src_ref=src,
            dst_ref=dst,
            send_sem=send_sem.at[side, c],
            recv_sem=recv_sem.at[land, c],
            device_id=target[side],
            device_id_type=MESH,
        )

    def stream_copy(step, land):
        to = lax.rem(s + step, NS)
        return pltpu.make_async_remote_copy(
            src_ref=send_1.at[to],
            dst_ref=arrived_1.at[pl.ds(land * PACK_1, PACK_1)],
            send_sem=send_sem_1.at[step],
            recv_sem=recv_sem_1.at[land],
            device_id=(to, g),
            device_id_type=MESH,
        )

    def girth_copy(step, land):
        to = lax.rem(g + step, NG)
        return pltpu.make_async_remote_copy(
            src_ref=send_2.at[to],
            dst_ref=arrived_2.at[land],
            send_sem=send_sem_2.at[step],
            recv_sem=recv_sem_2.at[land],
            device_id=(s, to),
            device_id_type=MESH,
        )

    for copy in singles[:5]:
        copy.start()
    for c in range(PAIRS):
        it_copy(c).start()
    for copy in singles[5:]:
        copy.start()
    for c in range(PAIRS):
        rhs_copy(c).start()

    barrier = pltpu.get_barrier_semaphore()
    for step in range(1, NS):
        pl.semaphore_signal(
            barrier, inc=1, device_id=(lax.rem(s + step, NS), g), device_id_type=MESH
        )
    for step in range(1, NG):
        pl.semaphore_signal(
            barrier, inc=1, device_id=(s, lax.rem(g + step, NG)), device_id_type=MESH
        )

    for side in range(4):

        @pl.when(jnp.logical_not(present[side]))
        def _():
            if side in (WEST, EAST):
                halo_x[side] = jnp.zeros((V, K, CG, NR), F32)
            else:
                halo_g[side - 2] = jnp.zeros((V, K, CX, NR), F32)

    for copy in singles[:5]:
        copy.wait()

    turns = (0, 0, 7, 1, 0, 0)
    wmain[...] = jnp.concatenate(
        [operator(jac[f], turns[f]) for f in range(6)], axis=0
    ).astype(BF16)
    pad = jnp.zeros((64 - BLK, DEPTH), F32)
    for f in range(4):
        wside[f] = jnp.concatenate([operator(jac[f], 0), pad], axis=0).astype(BF16)

    pl.semaphore_wait(barrier, NS + NG - 2)

    for c in range(PAIRS):
        for side in (WEST, EAST):

            @pl.when(present[side])
            def _():
                halo_copy(side, c).start()

    for c in range(PAIRS):
        it_copy(c).wait()
        for k in (2 * c, 2 * c + 1):
            for v in range(V):
                send_g[0, v, k] = it_v[v, k, pl.ds(0, CX, stride=CG), :]
                send_g[1, v, k] = it_v[v, k, pl.ds(CG - 1, CX, stride=CG), :]

        for side in (SOUTH, NORTH):

            @pl.when(present[side])
            def _():
                halo_copy(side, c).start()

    names = (owner[...] == lax.broadcasted_iota(jnp.int32, (DEV, SLOTS), 0)).astype(F32)
    r = lax.broadcasted_iota(jnp.int32, (SLOTS, SLOTS), 0)
    c = lax.broadcasted_iota(jnp.int32, (SLOTS, SLOTS), 1)
    earlier = jnp.dot(names.astype(BF16), (r < c).astype(BF16), preferred_element_type=F32)
    place = jnp.sum(names * earlier, axis=0, keepdims=True).astype(jnp.int32)

    for copy in singles[5:]:
        copy.wait()

    sub = lax.broadcasted_iota(jnp.int32, (8, NR), 0)
    lane = lax.broadcasted_iota(jnp.int32, (8, NR), 1)

    def main(c):
        k0 = 2 * c

        def rows(x, t):
            return pl.ds(x * CG + 8 * t, 8)

        def pair(ref, *at):
            return jnp.concatenate([ref[at[0], k0 + j, *at[1:]] for j in range(2)], axis=1)

        def finish(x, left, image):
            for t in range(2):
                w = fw_v[1, rows(x, t), :]
                rem = [
                    [left[t][j][u] - w * image[t][u * 8 : u * 8 + 8, j * NR : (j + 1) * NR] for u in range(V)]
                    for j in range(2)
                ]
                for u in range(V):
                    acc = [None, None]
                    for v in range(V):
                        b = binv_v[u, v, rows(x, t), :]
                        for j in range(2):
                            term = b * rem[j][v]
                            acc[j] = term if acc[j] is None else acc[j] + term
                    for j in range(2):
                        upd[u, k0 + j, rows(x, t), :] = acc[j]

        def outer(side, t):
            return jnp.dot(
                wside[side],
                operand(lambda v: pair(halo_x.at[side], v, pl.ds(8 * t, 8))),
                preferred_element_type=F32,
            )

        for side in range(2):
            edge[side] = jnp.dot(
                wside[2 + side],
                operand(lambda v: pair(halo_g.at[side], v)),
                preferred_element_type=F32,
            )
        before, left_before = [outer(WEST, t) for t in range(2)], None
        for x in range(CX):
            y = [
                jnp.dot(
                    wmain[...],
                    operand(lambda v, t=t: pair(it_v, v, rows(x, t))),
                    preferred_element_type=F32,
                )
                for t in range(2)
            ]

            def part(t, f, u, j):
                at = f * BLK + u * 8
                return y[t][at : at + 8, j * NR : (j + 1) * NR]

            w = [[fw_v[f, rows(x, t), :] for f in range(6)] for t in range(2)]
            for t in range(2):
                w[t][4] = jnp.where(lane == 0, 0.0, w[t][4])
                w[t][5] = jnp.where(lane == NR - 1, 0.0, w[t][5])
            left = [[[None] * V for _ in range(2)] for _ in range(2)]
            for t in range(2):
                for j in range(2):
                    for u in range(V):
                        at = u * 8 + x
                        if t == 0:
                            first = edge[0, at : at + 1, j * NR : (j + 1) * NR]
                            last = part(1, 3, u, j)
                        else:
                            first = part(0, 2, u, j)
                            last = edge[1, at : at + 1, j * NR : (j + 1) * NR]
                        y2 = jnp.where(sub == 0, first, part(t, 2, u, j))
                        y3 = jnp.where(sub == 7, last, part(t, 3, u, j))
                        total = w[t][2] * y2 + w[t][3] * y3
                        total += w[t][4] * pltpu.roll(part(t, 4, u, j), 1, axis=1)
                        total += w[t][5] * pltpu.roll(part(t, 5, u, j), NR - 1, axis=1)
                        total += w[t][0] * before[t][u * 8 : u * 8 + 8, j * NR : (j + 1) * NR]
                        left[t][j][u] = rhs_v[u, k0 + j, rows(x, t), :] - total
            if x > 0:
                finish(x - 1, left_before, [y[t][BLK : 2 * BLK] for t in range(2)])
            before, left_before = [y[t][0:BLK] for t in range(2)], left
        finish(CX - 1, left_before, [outer(EAST, t) for t in range(2)])

    r = lax.broadcasted_iota(jnp.int32, (2 * NR, SLOTS), 0)
    lanes = (cell[...] % NR == r % NR).astype(BF16)
    r = lax.broadcasted_iota(jnp.int32, (ROWS, SLOTS), 0)
    on_row = (cell[...] // NR == r).astype(F32)

    @pl.loop(0, PAIRS)
    def _(c):
        rhs_copy(c).wait()
        for side in range(4):

            @pl.when(present[side])
            def _():
                halo_copy(side, c, side).wait_recv()

        main(c)
        for j in range(2):
            hi, lo = split(upd[0, 2 * c + j])
            both = jnp.concatenate([hi, lo], axis=1).astype(BF16)
            found = jnp.dot(both, lanes, preferred_element_type=F32) * on_row
            pick[pl.ds(2 * c + j, 1), :] = jnp.sum(found, axis=0, keepdims=True)

    pressure = pick[...]
    shapes = shape[...]
    values = jnp.concatenate(
        [pressure, shapes, jnp.broadcast_to(patch[...].astype(F32), (8, SLOTS))], axis=0
    )
    spread = jnp.concatenate([values] * 4, axis=0)
    group = lax.broadcasted_iota(jnp.int32, (NR, SLOTS), 0) // 32
    chosen = names.astype(BF16)
    chosen = jnp.concatenate([chosen, chosen], axis=1)
    for half in range(2):
        hi, lo = split(jnp.where(place == 4 * half + group, spread, 0.0))
        packed = nt(chosen, jnp.concatenate([hi, lo], axis=1).astype(BF16))
        send_1[:, NG * half : NG * (half + 1), :] = packed.reshape(NS, NG, NR)
    products = jnp.concatenate([shapes[m : m + 1] * pressure for m in range(8)], axis=0)
    sums = nt(jnp.ones((8, SLOTS), F32), products, HIGH)
    send_1[:, 2 * NG :, :] = jnp.broadcast_to(sums[None], (NS, 8, NR))

    for step in range(1, NS):
        stream_copy(step, s).start()
    arrived_1[pl.ds(pl.multiple_of(s * PACK_1, 8), PACK_1), :] = send_1[s]
    for step in range(1, NS):
        stream_copy(step, lax.rem(s + NS - step, NS)).wait_recv()
    for to in range(NG):
        for half in range(2):
            send_2[to, 8 * half : 8 * half + 8, :] = arrived_1[
                pl.ds(half * NG + to, NS, stride=PACK_1), :
            ]
    sums = jnp.sum(arrived_1[pl.ds(2 * NG, NS, stride=PACK_1), :], axis=0, keepdims=True)
    send_2[:, 16:, :] = jnp.broadcast_to(sums[None], (NG, 8, NR))
    for step in range(1, NG):
        girth_copy(step, g).start()
    arrived_2[g] = send_2[g]
    for step in range(1, NG):
        girth_copy(step, lax.rem(g + NG - step, NG)).wait_recv()
    arrived_out[...] = arrived_2[...]

    for c in range(PAIRS):
        for side in range(4):

            @pl.when(present[side])
            def _():
                halo_copy(side, c).wait_send()

    for step in range(1, NS):
        stream_copy(step, s).wait_send()
    for step in range(1, NG):
        girth_copy(step, g).wait_send()


def force_kernel(upd, arrived, upd_out, patch_out, force_out, patch_force, force, sem):
    copies = [
        pltpu.make_async_copy(upd.at[v], upd_out.at[v], sem.at[v]) for v in range(V)
    ]
    for copy in copies:
        copy.start()

    lane = lax.broadcasted_iota(jnp.int32, (2 * NR, NR), 0) % NR
    column = lax.broadcasted_iota(jnp.int32, (2 * NR, NR), 1)
    patch = lax.broadcasted_iota(jnp.int32, (DEV, NR), 1).astype(F32)
    total = None
    for half in range(2):
        hi, lo = split(arrived[:, 8 * half : 8 * half + 8, :].reshape(DEV, NR))
        both = jnp.concatenate([hi, lo], axis=1).astype(BF16)
        for j in range(4):
            base = 32 * j
            by_shape = (lane == base + K + column // K).astype(BF16)
            by_rhs = (lane == base + column % K).astype(BF16)
            by_patch = (lane == base + 24).astype(BF16)
            contribution = jnp.dot(both, by_shape, preferred_element_type=F32) * jnp.dot(
                both, by_rhs, preferred_element_type=F32
            )
            label = jnp.dot(both, by_patch, preferred_element_type=F32)
            member = (label == patch).astype(F32).T[0:PATCH_DEV].astype(BF16)
            hi, lo = split(contribution)
            term = jnp.dot(member, hi.astype(BF16), preferred_element_type=F32) + jnp.dot(
                member, lo.astype(BF16), preferred_element_type=F32
            )
            total = term if total is None else total + term
    patch_force[...] = total
    out_patch = pltpu.make_async_copy(patch_force, patch_out, sem.at[V])
    out_patch.start()
    sums = jnp.sum(arrived[:, 16, :], axis=0, keepdims=True) / jnp.sqrt(F32(DEV * SLOTS))
    r = lax.broadcasted_iota(jnp.int32, (8, NR), 0)
    c = lax.broadcasted_iota(jnp.int32, (8, NR), 1)
    rows = jnp.where(c // K == r, sums, 0.0)
    r = lax.broadcasted_iota(jnp.int32, (K, NR), 0)
    c = lax.broadcasted_iota(jnp.int32, (K, NR), 1)
    force[...] = nt(rows, (c % K == r).astype(F32), HIGH)
    out_force = pltpu.make_async_copy(force, force_out, sem.at[V + 1])
    out_force.start()
    for copy in copies:
        copy.wait()
    out_patch.wait()
    out_force.wait()


def shards(iterate, right_side, block_inverse, face_weight, face_jacobian, wall_cell, wall_owner, wall_patch, wall_shape):
    hbm = pl.BlockSpec(memory_space=pltpu.HBM)
    vmem = pl.BlockSpec(memory_space=pltpu.VMEM)
    dma = pltpu.SemaphoreType.DMA
    operands = (
        iterate.reshape(V, K, ROWS, NR),
        right_side.reshape(V, K, ROWS, NR),
        block_inverse.reshape(V, V, ROWS, NR),
        face_weight.reshape(6, ROWS, NR),
        face_jacobian,
        wall_cell.reshape(1, SLOTS),
        wall_owner.reshape(1, SLOTS),
        wall_patch.reshape(1, SLOTS),
        wall_shape.T,
    )
    updated, arrived = pl.pallas_call(
        sweep_kernel,
        out_shape=(
            pltpu.VMEM((V, K, ROWS, NR), F32),
            pltpu.VMEM((NG, 24, NR), F32),
        ),
        in_specs=[hbm] * 9,
        out_specs=(vmem, vmem),
        scratch_shapes=[
            pltpu.VMEM((V, K, ROWS, NR), F32),
            pltpu.VMEM((V, K, ROWS, NR), F32),
            pltpu.VMEM((V, V, ROWS, NR), F32),
            pltpu.VMEM((6, ROWS, NR), F32),
            pltpu.VMEM((2, V, K, CG, NR), F32),
            pltpu.VMEM((2, V, K, CX, NR), F32),
            pltpu.VMEM((2, V, K, CX, NR), F32),
            pltpu.VMEM((6 * BLK, DEPTH), BF16),
            pltpu.VMEM((4, 64, DEPTH), BF16),
            pltpu.VMEM((2, 64, 2 * NR), F32),
            pltpu.VMEM((K, SLOTS), F32),
            pltpu.VMEM((6, V, V), F32),
            pltpu.VMEM((1, SLOTS), jnp.int32),
            pltpu.VMEM((1, SLOTS), jnp.int32),
            pltpu.VMEM((1, SLOTS), jnp.int32),
            pltpu.VMEM((8, SLOTS), F32),
            pltpu.VMEM((NS, PACK_1, NR), F32),
            pltpu.VMEM((NS * PACK_1, NR), F32),
            pltpu.VMEM((NG, 24, NR), F32),
            pltpu.VMEM((NG, 24, NR), F32),
            dma((PAIRS,)),
            dma((PAIRS,)),
            dma((7,)),
            dma((4, PAIRS)),
            dma((4, PAIRS)),
            dma((NS,)),
            dma((NS,)),
            dma((NG,)),
            dma((NG,)),
        ],
        compiler_params=pltpu.CompilerParams(
            collective_id=0, has_side_effects=True, vmem_limit_bytes=32 * 1024 * 1024
        ),
    )(*[pltpu.with_memory_space_constraint(x, pltpu.HBM) for x in operands])
    updated, patch_force, force = pl.pallas_call(
        force_kernel,
        out_shape=(
            pltpu.HBM((V, K, ROWS, NR), F32),
            pltpu.HBM((PATCH_DEV, NR), F32),
            pltpu.HBM((8, K), F32),
        ),
        in_specs=[vmem, vmem],
        out_specs=(hbm, hbm, hbm),
        scratch_shapes=[
            pltpu.VMEM((PATCH_DEV, NR), F32),
            pltpu.VMEM((8, K), F32),
            dma((V + 2,)),
        ],
        compiler_params=pltpu.CompilerParams(vmem_limit_bytes=8 * 1024 * 1024),
    )(
        pltpu.with_memory_space_constraint(updated, pltpu.VMEM),
        pltpu.with_memory_space_constraint(arrived, pltpu.VMEM),
    )
    return (updated.reshape(V, K, CX, CG, NR), patch_force, force)


def solution(mesh):
    placed = (
        P(None, None, "stream", "girth", None),
        P(None, None, "stream", "girth", None),
        P(None, None, "stream", "girth", None),
        P(None, "stream", "girth", None),
        P(),
        P(("stream", "girth")),
        P(("stream", "girth"), None),
        P(("stream", "girth")),
        P(("stream", "girth"), None),
    )
    return jax.shard_map(
        shards,
        mesh=mesh,
        in_specs=placed,
        out_specs=(P(None, None, "stream", "girth", None), P(("stream", "girth"), None), P()),
        check_vma=False,
    )
```

```python
import jax
import jax.numpy as jnp
from jax import lax
from jax.experimental import pallas as pl
from jax.experimental.pallas import tpu as pltpu
from jax.sharding import PartitionSpec as P

V = 7
K = 16
CX = 8
CG = 16
NR = 128
ROWS = CX * CG
SLOTS = 256
PATCH_DEV = 32
NS = 8
NG = 16
DEV = NS * NG
PAIRS = K // 2
PACK_1 = 2 * NG + 8
REST_1 = 32
BLK = V * 8
TERM = 64
DEPTH = 3 * TERM
MESH = pl.DeviceIdType.MESH
HIGH = lax.Precision.HIGHEST
F32 = jnp.float32
BF16 = jnp.bfloat16
WEST, EAST, SOUTH, NORTH = range(4)


def nt(a, b, precision=None):
    return lax.dot_general(
        a, b, (((1,), (1,)), ((), ())), precision=precision, preferred_element_type=F32
    )


def split(x):
    hi = x.astype(BF16).astype(F32)
    return hi, x - hi


def operator(jacobian, turn):
    r = lax.broadcasted_iota(jnp.int32, (BLK, V), 0)
    c = lax.broadcasted_iota(jnp.int32, (BLK, V), 1)
    rows = (r // 8 == c).astype(F32)
    r = lax.broadcasted_iota(jnp.int32, (V, DEPTH), 0)
    c = lax.broadcasted_iota(jnp.int32, (V, DEPTH), 1)
    columns = ((c % TERM) // 8 == r).astype(F32)
    spread = jnp.dot(jnp.dot(rows, jacobian, precision=HIGH), columns, precision=HIGH)
    hi, lo = split(spread)
    r = lax.broadcasted_iota(jnp.int32, (BLK, DEPTH), 0)
    c = lax.broadcasted_iota(jnp.int32, (BLK, DEPTH), 1)
    keep = (r + turn) % 8 == c % 8
    return jnp.where(keep, jnp.where(c < 2 * TERM, hi, lo), 0.0)


def operand(load):
    pad = jnp.zeros((TERM - BLK, 2 * NR), F32)
    x = jnp.concatenate([load(v) for v in range(V)] + [pad], axis=0)
    hi = x.astype(BF16)
    lo = (x - hi.astype(F32)).astype(BF16)
    return jnp.concatenate([hi, lo, hi], axis=0)


def sweep_kernel(
    it, rhs, binv, fw, jac_in, cell_in, owner_in, patch_in, shape_in,
    upd, arrived_out,
    it_v, rhs_v, binv_v, fw_v, halo_x, halo_g, send_g, wmain, wside, pick,
    jac, cell, owner, patch, shape, send_1, arrived_1, send_2, arrived_2,
    sem_it, sem_rhs, sem_misc, send_sem, recv_sem, send_sem_1, recv_sem_1, send_sem_2, recv_sem_2, relay,
):
    s, g = lax.axis_index("stream"), lax.axis_index("girth")
    present = (s > 0, s < NS - 1, g > 0, g < NG - 1)
    target = ((s - 1, g), (s + 1, g), (s, g - 1), (s, g + 1))

    def it_copy(c):
        ks = pl.ds(2 * c, 2)
        return pltpu.make_async_copy(it.at[:, ks], it_v.at[:, ks], sem_it.at[c])

    def rhs_copy(c):
        ks = pl.ds(2 * c, 2)
        return pltpu.make_async_copy(rhs.at[:, ks], rhs_v.at[:, ks], sem_rhs.at[c])

    singles = [
        pltpu.make_async_copy(a, b, sem_misc.at[i])
        for i, (a, b) in enumerate(
            (
                (jac_in, jac),
                (cell_in, cell),
                (owner_in, owner),
                (patch_in, patch),
                (shape_in, shape),
                (fw, fw_v),
                (binv, binv_v),
            )
        )
    ]

    def halo_copy(side, c, land=None):
        land = side ^ 1 if land is None else land
        ks = pl.ds(2 * c, 2)
        if side in (WEST, EAST):
            rows = pl.ds(0 if side == WEST else ROWS - CG, CG)
            src, dst = it_v.at[:, ks, rows], halo_x.at[land, :, ks]
        else:
            src, dst = send_g.at[side - 2, :, ks], halo_g.at[land - 2, :, ks]
        return pltpu.make_async_remote_copy(
            src_ref=src,
            dst_ref=dst,
            send_sem=send_sem.at[side, c],
            recv_sem=recv_sem.at[land, c],
            device_id=target[side],
            device_id_type=MESH,
        )

    def stream_copy(step, land):
        to = lax.rem(s + step, NS)
        return pltpu.make_async_remote_copy(
            src_ref=send_1.at[to],
            dst_ref=arrived_1.at[pl.ds(land * PACK_1, PACK_1)],
            send_sem=send_sem_1.at[step],
            recv_sem=recv_sem_1.at[land],
            device_id=(to, g),
            device_id_type=MESH,
        )

    def girth_copy(step, land):
        to = lax.rem(g + step, NG)
        return pltpu.make_async_remote_copy(
            src_ref=send_2.at[to],
            dst_ref=arrived_2.at[land],
            send_sem=send_sem_2.at[step],
            recv_sem=recv_sem_2.at[land],
            device_id=(s, to),
            device_id_type=MESH,
        )

    def ring(axis, step):
        if axis == 0:
            return (lax.rem(s + step + NS, NS), g)
        return (s, lax.rem(g + step + NG, NG))

    def relay_signal(axis, level):
        for way in range(2):
            pl.semaphore_signal(
                relay.at[axis, level, way],
                inc=1,
                device_id=ring(axis, (1 << level) * (1 - 2 * way)),
                device_id_type=MESH,
            )

    def relay_wait(axis, level):
        for way in range(2):
            pl.semaphore_wait(relay.at[axis, level, way], 1)

    barrier = pltpu.get_barrier_semaphore()
    for axis in range(2):
        for step in (1, -1):
            pl.semaphore_signal(barrier, inc=1, device_id=ring(axis, step), device_id_type=MESH)

    for copy in singles[:5]:
        copy.start()
    for c in range(PAIRS):
        it_copy(c).start()
    for copy in singles[5:]:
        copy.start()
    for c in range(PAIRS):
        rhs_copy(c).start()

    for side in range(4):

        @pl.when(jnp.logical_not(present[side]))
        def _():
            if side in (WEST, EAST):
                halo_x[side] = jnp.zeros((V, K, CG, NR), F32)
            else:
                halo_g[side - 2] = jnp.zeros((V, K, CX, NR), F32)

    for copy in singles[:5]:
        copy.wait()

    turns = (0, 0, 7, 1, 0, 0)
    parts = [operator(jac[f], turns[f]) for f in range(6)]
    wmain[...] = jnp.concatenate(
        [parts[f][8 * u : 8 * u + 8] for u in range(V) for f in range(6)], axis=0
    ).astype(BF16)
    pad = jnp.zeros((TERM - BLK, DEPTH), F32)
    for f in range(4):
        wside[f] = jnp.concatenate([operator(jac[f], 0), pad], axis=0).astype(BF16)

    for c in range(PAIRS):
        it_copy(c).wait()
        for k in (2 * c, 2 * c + 1):
            for v in range(V):
                send_g[0, v, k] = it_v[v, k, pl.ds(0, CX, stride=CG), :]
                send_g[1, v, k] = it_v[v, k, pl.ds(CG - 1, CX, stride=CG), :]

    pl.semaphore_wait(barrier, 4)

    for c in range(PAIRS):
        for side in range(4):

            @pl.when(present[side])
            def _():
                halo_copy(side, c).start()

    relay_signal(0, 0)
    relay_signal(1, 0)

    names = (owner[...] == lax.broadcasted_iota(jnp.int32, (DEV, SLOTS), 0)).astype(F32)
    r = lax.broadcasted_iota(jnp.int32, (SLOTS, SLOTS), 0)
    c = lax.broadcasted_iota(jnp.int32, (SLOTS, SLOTS), 1)
    earlier = jnp.dot(names.astype(BF16), (r < c).astype(BF16), preferred_element_type=F32)
    place = jnp.sum(names * earlier, axis=0, keepdims=True).astype(jnp.int32)

    for copy in singles[5:]:
        copy.wait()

    sub = lax.broadcasted_iota(jnp.int32, (8, NR), 0)
    lane = lax.broadcasted_iota(jnp.int32, (8, NR), 1)

    def rows(x, t):
        return pl.ds(x * CG + 8 * t, 8)

    def borders(c):
        k0 = 2 * c
        for side in range(4):
            for t in range(2 if side in (WEST, EAST) else 1):
                if side in (WEST, EAST):
                    at = rows(0 if side == WEST else CX - 1, t)

                    def load(v):
                        return jnp.concatenate(
                            [halo_x[side, v, k0 + j, pl.ds(8 * t, 8), :] for j in range(2)], axis=1
                        )
                else:
                    at = pl.ds(0 if side == SOUTH else CG - 1, CX, stride=CG)

                    def load(v):
                        return jnp.concatenate([halo_g[side - 2, v, k0 + j] for j in range(2)], axis=1)

                z = jnp.dot(wside[side], operand(load), preferred_element_type=F32)
                w = fw_v[side, at, :]
                for u in range(V):
                    for j in range(2):
                        image = z[u * 8 : u * 8 + 8, j * NR : (j + 1) * NR]
                        rhs_v[u, k0 + j, at, :] = rhs_v[u, k0 + j, at, :] - w * image

    def main(c):
        k0 = 2 * c

        def finish(x, left):
            for t in range(2):
                for j in range(2):
                    acc = None
                    for v in range(V):
                        rhs_v[v, k0 + j, rows(x, t), :] = left[t][j][v]
                        term = binv_v[0, v, rows(x, t), :] * left[t][j][v]
                        acc = term if acc is None else acc + term
                    upd[0, k0 + j, rows(x, t), :] = acc

        before, left_before = None, None
        for x in range(CX):
            y = [
                jnp.dot(
                    wmain[...],
                    operand(
                        lambda v, t=t: jnp.concatenate(
                            [it_v[v, k0 + j, rows(x, t), :] for j in range(2)], axis=1
                        )
                    ),
                    preferred_element_type=F32,
                )
                for t in range(2)
            ]

            def part(t, f, u, j):
                at = (u * 6 + f) * 8
                return y[t][at : at + 8, j * NR : (j + 1) * NR]

            w = [[fw_v[f, rows(x, t), :] for f in range(6)] for t in range(2)]
            w[0][2] = jnp.where(sub == 0, 0.0, w[0][2])
            w[1][3] = jnp.where(sub == 7, 0.0, w[1][3])
            for t in range(2):
                w[t][4] = jnp.where(lane == 0, 0.0, w[t][4])
                w[t][5] = jnp.where(lane == NR - 1, 0.0, w[t][5])
            left = [[[None] * V for _ in range(2)] for _ in range(2)]
            kept = [[[None] * V for _ in range(2)] for _ in range(2)]
            for u in range(V):
                for t in range(2):
                    for j in range(2):
                        y2, y3 = part(t, 2, u, j), part(t, 3, u, j)
                        if t == 1:
                            y2 = jnp.where(sub == 0, part(0, 2, u, j), y2)
                        else:
                            y3 = jnp.where(sub == 7, part(1, 3, u, j), y3)
                        total = w[t][2] * y2 + w[t][3] * y3
                        total += w[t][4] * pltpu.roll(part(t, 4, u, j), 1, axis=1)
                        total += w[t][5] * pltpu.roll(part(t, 5, u, j), NR - 1, axis=1)
                        if x > 0:
                            total += w[t][0] * before[t][j][u]
                            left_before[t][j][u] = left_before[t][j][u] - fw_v[1, rows(x - 1, t), :] * part(t, 1, u, j)
                        left[t][j][u] = rhs_v[u, k0 + j, rows(x, t), :] - total
                        kept[t][j][u] = part(t, 0, u, j)
            if x > 0:
                finish(x - 1, left_before)
            before, left_before = kept, left
        finish(CX - 1, left_before)

    def rest(first, last):
        @pl.loop(first, last)
        def _(i):
            k0, x = 2 * (i // CX), i % CX
            for t in range(2):
                at = pl.ds(pl.multiple_of(x * CG + 8 * t, 8), 8)
                rem = [[rhs_v[v, k0 + j, at, :] for v in range(V)] for j in range(2)]
                for u in range(1, V):
                    acc = [None, None]
                    for v in range(V):
                        b = binv_v[u, v, at, :]
                        for j in range(2):
                            term = b * rem[j][v]
                            acc[j] = term if acc[j] is None else acc[j] + term
                    for j in range(2):
                        upd[u, k0 + j, at, :] = acc[j]

    r = lax.broadcasted_iota(jnp.int32, (2 * NR, SLOTS), 0)
    lanes = (cell[...] % NR == r % NR).astype(BF16)
    r = lax.broadcasted_iota(jnp.int32, (ROWS, SLOTS), 0)
    on_row = (cell[...] // NR == r).astype(F32)

    @pl.loop(0, PAIRS)
    def _(c):
        rhs_copy(c).wait()
        for side in range(4):

            @pl.when(present[side])
            def _():
                halo_copy(side, c, side).wait_recv()

        for at, done, then in ((1, ((0, 0), (1, 0)), ((0, 1), (1, 1))), (3, ((0, 1), (1, 1)), ((1, 2),)), (5, ((1, 2),), ())):

            @pl.when(c == at)
            def _():
                for axis, level in done:
                    relay_wait(axis, level)
                for axis, level in then:
                    relay_signal(axis, level)

        borders(c)
        main(c)
        for j in range(2):
            hi, lo = split(upd[0, 2 * c + j])
            both = jnp.concatenate([hi, lo], axis=1).astype(BF16)
            found = jnp.dot(both, lanes, preferred_element_type=F32) * on_row
            pick[pl.ds(2 * c + j, 1), :] = jnp.sum(found, axis=0, keepdims=True)

    pressure = pick[...]
    shapes = shape[...]
    values = jnp.concatenate(
        [pressure, shapes, jnp.broadcast_to(patch[...].astype(F32), (8, SLOTS))], axis=0
    )
    spread = jnp.concatenate([values] * 4, axis=0)
    group = lax.broadcasted_iota(jnp.int32, (NR, SLOTS), 0) // 32
    chosen = names.astype(BF16)
    chosen = jnp.concatenate([chosen, chosen], axis=1)
    for half in range(2):
        hi, lo = split(jnp.where(place == 4 * half + group, spread, 0.0))
        packed = nt(chosen, jnp.concatenate([hi, lo], axis=1).astype(BF16))
        send_1[:, NG * half : NG * (half + 1), :] = packed.reshape(NS, NG, NR)
    products = jnp.concatenate([shapes[m : m + 1] * pressure for m in range(8)], axis=0)
    sums = nt(jnp.ones((8, SLOTS), F32), products, HIGH)
    send_1[:, 2 * NG :, :] = jnp.broadcast_to(sums[None], (NS, 8, NR))

    for step in range(1, NS):
        stream_copy(step, s).start()
    arrived_1[pl.ds(pl.multiple_of(s * PACK_1, 8), PACK_1), :] = send_1[s]
    rest(0, REST_1)
    for step in range(1, NS):
        stream_copy(step, lax.rem(s + NS - step, NS)).wait_recv()
    for to in range(NG):
        for half in range(2):
            send_2[to, 8 * half : 8 * half + 8, :] = arrived_1[
                pl.ds(half * NG + to, NS, stride=PACK_1), :
            ]
    sums = jnp.sum(arrived_1[pl.ds(2 * NG, NS, stride=PACK_1), :], axis=0, keepdims=True)
    send_2[:, 16:, :] = jnp.broadcast_to(sums[None], (NG, 8, NR))
    for step in range(1, NG):
        girth_copy(step, g).start()
    arrived_2[g] = send_2[g]
    rest(REST_1, PAIRS * CX)
    for step in range(1, NG):
        girth_copy(step, lax.rem(g + NG - step, NG)).wait_recv()
    arrived_out[...] = arrived_2[...]

    for c in range(PAIRS):
        for side in range(4):

            @pl.when(present[side])
            def _():
                halo_copy(side, c).wait_send()

    for step in range(1, NS):
        stream_copy(step, s).wait_send()
    for step in range(1, NG):
        girth_copy(step, g).wait_send()


def force_kernel(upd, arrived, upd_out, patch_out, force_out, patch_force, force, sem):
    copies = [
        pltpu.make_async_copy(upd.at[v], upd_out.at[v], sem.at[v]) for v in range(V)
    ]
    for copy in copies:
        copy.start()

    lane = lax.broadcasted_iota(jnp.int32, (2 * NR, NR), 0) % NR
    column = lax.broadcasted_iota(jnp.int32, (2 * NR, NR), 1)
    patch = lax.broadcasted_iota(jnp.int32, (DEV, NR), 1).astype(F32)
    total = None
    for half in range(2):
        hi, lo = split(arrived[:, 8 * half : 8 * half + 8, :].reshape(DEV, NR))
        both = jnp.concatenate([hi, lo], axis=1).astype(BF16)
        for j in range(4):
            base = 32 * j
            by_shape = (lane == base + K + column // K).astype(BF16)
            by_rhs = (lane == base + column % K).astype(BF16)
            by_patch = (lane == base + 24).astype(BF16)
            contribution = jnp.dot(both, by_shape, preferred_element_type=F32) * jnp.dot(
                both, by_rhs, preferred_element_type=F32
            )
            label = jnp.dot(both, by_patch, preferred_element_type=F32)
            member = (label == patch).astype(F32).T[0:PATCH_DEV].astype(BF16)
            hi, lo = split(contribution)
            term = jnp.dot(member, hi.astype(BF16), preferred_element_type=F32) + jnp.dot(
                member, lo.astype(BF16), preferred_element_type=F32
            )
            total = term if total is None else total + term
    patch_force[...] = total
    out_patch = pltpu.make_async_copy(patch_force, patch_out, sem.at[V])
    out_patch.start()
    sums = jnp.sum(arrived[:, 16, :], axis=0, keepdims=True) / jnp.sqrt(F32(DEV * SLOTS))
    r = lax.broadcasted_iota(jnp.int32, (8, NR), 0)
    c = lax.broadcasted_iota(jnp.int32, (8, NR), 1)
    rows = jnp.where(c // K == r, sums, 0.0)
    r = lax.broadcasted_iota(jnp.int32, (K, NR), 0)
    c = lax.broadcasted_iota(jnp.int32, (K, NR), 1)
    force[...] = nt(rows, (c % K == r).astype(F32), HIGH)
    out_force = pltpu.make_async_copy(force, force_out, sem.at[V + 1])
    out_force.start()
    for copy in copies:
        copy.wait()
    out_patch.wait()
    out_force.wait()


def shards(iterate, right_side, block_inverse, face_weight, face_jacobian, wall_cell, wall_owner, wall_patch, wall_shape):
    hbm = pl.BlockSpec(memory_space=pltpu.HBM)
    vmem = pl.BlockSpec(memory_space=pltpu.VMEM)
    dma = pltpu.SemaphoreType.DMA
    operands = (
        iterate.reshape(V, K, ROWS, NR),
        right_side.reshape(V, K, ROWS, NR),
        block_inverse.reshape(V, V, ROWS, NR),
        face_weight.reshape(6, ROWS, NR),
        face_jacobian,
        wall_cell.reshape(1, SLOTS),
        wall_owner.reshape(1, SLOTS),
        wall_patch.reshape(1, SLOTS),
        wall_shape.T,
    )
    updated, arrived = pl.pallas_call(
        sweep_kernel,
        out_shape=(
            pltpu.VMEM((V, K, ROWS, NR), F32),
            pltpu.VMEM((NG, 24, NR), F32),
        ),
        in_specs=[hbm] * 9,
        out_specs=(vmem, vmem),
        scratch_shapes=[
            pltpu.VMEM((V, K, ROWS, NR), F32),
            pltpu.VMEM((V, K, ROWS, NR), F32),
            pltpu.VMEM((V, V, ROWS, NR), F32),
            pltpu.VMEM((6, ROWS, NR), F32),
            pltpu.VMEM((2, V, K, CG, NR), F32),
            pltpu.VMEM((2, V, K, CX, NR), F32),
            pltpu.VMEM((2, V, K, CX, NR), F32),
            pltpu.VMEM((6 * BLK, DEPTH), BF16),
            pltpu.VMEM((4, TERM, DEPTH), BF16),
            pltpu.VMEM((K, SLOTS), F32),
            pltpu.VMEM((6, V, V), F32),
            pltpu.VMEM((1, SLOTS), jnp.int32),
            pltpu.VMEM((1, SLOTS), jnp.int32),
            pltpu.VMEM((1, SLOTS), jnp.int32),
            pltpu.VMEM((8, SLOTS), F32),
            pltpu.VMEM((NS, PACK_1, NR), F32),
            pltpu.VMEM((NS * PACK_1, NR), F32),
            pltpu.VMEM((NG, 24, NR), F32),
            pltpu.VMEM((NG, 24, NR), F32),
            dma((PAIRS,)),
            dma((PAIRS,)),
            dma((7,)),
            dma((4, PAIRS)),
            dma((4, PAIRS)),
            dma((NS,)),
            dma((NS,)),
            dma((NG,)),
            dma((NG,)),
            pltpu.SemaphoreType.REGULAR((2, 3, 2)),
        ],
        compiler_params=pltpu.CompilerParams(
            collective_id=0, has_side_effects=True, vmem_limit_bytes=32 * 1024 * 1024
        ),
    )(*[pltpu.with_memory_space_constraint(x, pltpu.HBM) for x in operands])
    updated, patch_force, force = pl.pallas_call(
        force_kernel,
        out_shape=(
            pltpu.HBM((V, K, ROWS, NR), F32),
            pltpu.HBM((PATCH_DEV, NR), F32),
            pltpu.HBM((8, K), F32),
        ),
        in_specs=[vmem, vmem],
        out_specs=(hbm, hbm, hbm),
        scratch_shapes=[
            pltpu.VMEM((PATCH_DEV, NR), F32),
            pltpu.VMEM((8, K), F32),
            dma((V + 2,)),
        ],
        compiler_params=pltpu.CompilerParams(vmem_limit_bytes=8 * 1024 * 1024),
    )(
        pltpu.with_memory_space_constraint(updated, pltpu.VMEM),
        pltpu.with_memory_space_constraint(arrived, pltpu.VMEM),
    )
    return (updated.reshape(V, K, CX, CG, NR), patch_force, force)


def solution(mesh):
    placed = (
        P(None, None, "stream", "girth", None),
        P(None, None, "stream", "girth", None),
        P(None, None, "stream", "girth", None),
        P(None, "stream", "girth", None),
        P(),
        P(("stream", "girth")),
        P(("stream", "girth"), None),
        P(("stream", "girth")),
        P(("stream", "girth"), None),
    )
    return jax.shard_map(
        shards,
        mesh=mesh,
        in_specs=placed,
        out_specs=(P(None, None, "stream", "girth", None), P(("stream", "girth"), None), P()),
        check_vma=False,
    )
```

```python
import jax
import jax.numpy as jnp
from jax import lax
from jax.experimental import pallas as pl
from jax.experimental.pallas import tpu as pltpu
from jax.sharding import PartitionSpec as P

V = 7
K = 16
CX = 8
CG = 16
NR = 128
ROWS = CX * CG
SLOTS = 256
PATCH_DEV = 32
NS = 8
NG = 16
DEV = NS * NG
PAIRS = K // 2
AHEAD = 3
HEARD = (1, 4)
BLK = V * 8
TERM = 64
DEPTH = 3 * TERM
MESH = pl.DeviceIdType.MESH
HIGH = lax.Precision.HIGHEST
F32 = jnp.float32
BF16 = jnp.bfloat16
WEST, EAST, SOUTH, NORTH = range(4)
STEPS = sorted(
    [(a, b, c, d) for a in range(4) for b in range(2) for c in range(4) for d in range(4)][1:],
    key=lambda o: -sum(min(n, 4 - n) for n in (o[0], o[2], o[3])),
)
NEAR = [(0, 1, 0, 0)] + [
    (n if a == 0 else 0, b, n if a == 1 else 0, n if a == 2 else 0)
    for a in range(3) for n in (1, 3) for b in range(2)
]
ROUNDS = (
    tuple(o for o in NEAR if o[1] == 0),
    tuple((n, 0, 0, 0) for n in (1, 2, 3)),
    tuple((0, 0, n, 0) for n in (1, 2, 3)),
)


def nt(a, b, precision=None):
    return lax.dot_general(
        a, b, (((1,), (1,)), ((), ())), precision=precision, preferred_element_type=F32
    )


def split(x):
    hi = x.astype(BF16).astype(F32)
    return hi, x - hi


def operator(jacobian, turn):
    r = lax.broadcasted_iota(jnp.int32, (BLK, V), 0)
    c = lax.broadcasted_iota(jnp.int32, (BLK, V), 1)
    rows = (r // 8 == c).astype(F32)
    r = lax.broadcasted_iota(jnp.int32, (V, DEPTH), 0)
    c = lax.broadcasted_iota(jnp.int32, (V, DEPTH), 1)
    columns = ((c % TERM) // 8 == r).astype(F32)
    spread = jnp.dot(jnp.dot(rows, jacobian, precision=HIGH), columns, precision=HIGH)
    hi, lo = split(spread)
    r = lax.broadcasted_iota(jnp.int32, (BLK, DEPTH), 0)
    c = lax.broadcasted_iota(jnp.int32, (BLK, DEPTH), 1)
    keep = (r + turn) % 8 == c % 8
    return jnp.where(keep, jnp.where(c < 2 * TERM, hi, lo), 0.0)


def operand(load):
    pad = jnp.zeros((TERM - BLK, 2 * NR), F32)
    x = jnp.concatenate([load(v) for v in range(V)] + [pad], axis=0)
    hi = x.astype(BF16)
    lo = (x - hi.astype(F32)).astype(BF16)
    return jnp.concatenate([hi, lo, hi], axis=0)


def sweep_kernel(
    it, rhs, binv, fw, jac_in, cell_in, owner_in, patch_in, shape_in,
    upd, arrived_out,
    it_v, rhs_v, binv_v, fw_v, halo_x, halo_g, send_g, wmain, wside, pick,
    jac, cell, owner, patch, shape, payload, arrived,
    sem_it, sem_rhs, sem_misc, send_sem, recv_sem, out_sem, in_sem, relay,
):
    s, g = lax.axis_index("stream"), lax.axis_index("girth")
    present = (s > 0, s < NS - 1, g > 0, g < NG - 1)
    target = ((s - 1, g), (s + 1, g), (s, g - 1), (s, g + 1))

    def it_copy(c):
        ks = pl.ds(2 * c, 2)
        return pltpu.make_async_copy(it.at[:, ks], it_v.at[:, ks], sem_it.at[c])

    def rhs_copy(c):
        ks = pl.ds(2 * c, 2)
        return pltpu.make_async_copy(rhs.at[:, ks], rhs_v.at[:, ks], sem_rhs.at[c])

    singles = [
        pltpu.make_async_copy(a, b, sem_misc.at[i])
        for i, (a, b) in enumerate(
            (
                (jac_in, jac),
                (cell_in, cell),
                (owner_in, owner),
                (patch_in, patch),
                (shape_in, shape),
                (fw, fw_v),
                (binv, binv_v),
            )
        )
    ]

    def halo_copy(side, c, land=None):
        land = side ^ 1 if land is None else land
        ks = pl.ds(2 * c, 2)
        if side in (WEST, EAST):
            rows = pl.ds(0 if side == WEST else ROWS - CG, CG)
            src, dst = it_v.at[:, ks, rows], halo_x.at[land, :, ks]
        else:
            src, dst = send_g.at[side - 2, :, ks], halo_g.at[land - 2, :, ks]
        return pltpu.make_async_remote_copy(
            src_ref=src,
            dst_ref=dst,
            send_sem=send_sem.at[side, c],
            recv_sem=recv_sem.at[land, c],
            device_id=target[side],
            device_id_type=MESH,
        )

    me = s * NG + g
    y, core, z, x4 = s // 2, lax.rem(s, 2), g // 4, lax.rem(g, 4)
    by_y = [2 * lax.rem(y + n, 4) for n in range(4)]
    by_core = [lax.rem(core + n, 2) for n in range(2)]
    by_z = [4 * lax.rem(z + n, 4) for n in range(4)]
    by_x = [lax.rem(x4 + n, 4) for n in range(4)]

    def at(step):
        return (by_y[step[0]] + by_core[step[1]], by_z[step[2]] + by_x[step[3]])

    def wall_copy(step):
        to = at(step)
        return pltpu.make_async_remote_copy(
            src_ref=payload.at[to[0] * NG + to[1]],
            dst_ref=arrived.at[me],
            send_sem=out_sem,
            recv_sem=in_sem,
            device_id=to,
            device_id_type=MESH,
        )

    others = pl.ds(0, DEV - 1)
    wall_all = pltpu.make_async_remote_copy(
        src_ref=payload.at[others],
        dst_ref=arrived.at[others],
        send_sem=out_sem,
        recv_sem=in_sem,
        device_id=(by_y[0] + by_core[1], g),
        device_id_type=MESH,
    )

    def relay_signal(level):
        for i, step in enumerate(ROUNDS[level]):
            pl.semaphore_signal(relay.at[level, i], inc=1, device_id=at(step), device_id_type=MESH)

    def relay_wait(level):
        for i in range(len(ROUNDS[level])):
            pl.semaphore_wait(relay.at[level, i], 1)

    for c in range(PAIRS):
        it_copy(c).start()

    barrier = pltpu.get_barrier_semaphore()
    for to in [at(step) for step in NEAR] + [(s, lax.rem(g + 1, NG)), (s, lax.rem(g + NG - 1, NG))]:
        pl.semaphore_signal(barrier, inc=1, device_id=to, device_id_type=MESH)

    for copy in singles:
        copy.start()
    for c in range(AHEAD):
        rhs_copy(c).start()

    for c in range(PAIRS):
        it_copy(c).wait()
        for k in (2 * c, 2 * c + 1):
            for v in range(V):
                send_g[0, v, k] = it_v[v, k, pl.ds(0, CX, stride=CG), :]
                send_g[1, v, k] = it_v[v, k, pl.ds(CG - 1, CX, stride=CG), :]
        if c == 3:
            pl.semaphore_wait(barrier, len(NEAR) + 2)
        for d in range(4) if c == 3 else ([c] if c > 3 else []):
            for side in range(4):

                @pl.when(present[side])
                def _():
                    halo_copy(side, d).start()

    relay_signal(0)
    for c in range(AHEAD, PAIRS):
        rhs_copy(c).start()

    for side in range(4):

        @pl.when(jnp.logical_not(present[side]))
        def _():
            if side in (WEST, EAST):
                halo_x[side] = jnp.zeros((V, K, CG, NR), F32)
            else:
                halo_g[side - 2] = jnp.zeros((V, K, CX, NR), F32)

    for copy in singles[:5]:
        copy.wait()

    turns = (0, 0, 7, 1, 0, 0)
    parts = [operator(jac[f], turns[f]) for f in range(6)]
    wmain[...] = jnp.concatenate(
        [parts[f][8 * u : 8 * u + 8] for u in range(V) for f in range(6)], axis=0
    ).astype(BF16)
    pad = jnp.zeros((TERM - BLK, DEPTH), F32)
    for f in range(4):
        wside[f] = jnp.concatenate([operator(jac[f], 0), pad], axis=0).astype(BF16)

    names = (owner[...] == lax.broadcasted_iota(jnp.int32, (DEV, SLOTS), 0)).astype(F32)
    r = lax.broadcasted_iota(jnp.int32, (SLOTS, SLOTS), 0)
    c = lax.broadcasted_iota(jnp.int32, (SLOTS, SLOTS), 1)
    earlier = jnp.dot(names.astype(BF16), (r < c).astype(BF16), preferred_element_type=F32)
    place = jnp.sum(names * earlier, axis=0, keepdims=True).astype(jnp.int32)

    for copy in singles[5:]:
        copy.wait()

    sub = lax.broadcasted_iota(jnp.int32, (8, NR), 0)
    lane = lax.broadcasted_iota(jnp.int32, (8, NR), 1)

    def rows(x, t):
        return pl.ds(x * CG + 8 * t, 8)

    def borders(c):
        k0 = 2 * c
        for side in range(4):
            for t in range(2 if side in (WEST, EAST) else 1):
                if side in (WEST, EAST):
                    at = rows(0 if side == WEST else CX - 1, t)

                    def load(v):
                        return jnp.concatenate(
                            [halo_x[side, v, k0 + j, pl.ds(8 * t, 8), :] for j in range(2)], axis=1
                        )
                else:
                    at = pl.ds(0 if side == SOUTH else CG - 1, CX, stride=CG)

                    def load(v):
                        return jnp.concatenate([halo_g[side - 2, v, k0 + j] for j in range(2)], axis=1)

                z = jnp.dot(wside[side], operand(load), preferred_element_type=F32)
                w = fw_v[side, at, :]
                for u in range(V):
                    for j in range(2):
                        image = z[u * 8 : u * 8 + 8, j * NR : (j + 1) * NR]
                        rhs_v[u, k0 + j, at, :] = rhs_v[u, k0 + j, at, :] - w * image

    def main(c):
        k0 = 2 * c

        def finish(x, left):
            for t in range(2):
                for j in range(2):
                    acc = None
                    for v in range(V):
                        rhs_v[v, k0 + j, rows(x, t), :] = left[t][j][v]
                        term = binv_v[0, v, rows(x, t), :] * left[t][j][v]
                        acc = term if acc is None else acc + term
                    upd[0, k0 + j, rows(x, t), :] = acc

        before, left_before = None, None
        for x in range(CX):
            y = [
                jnp.dot(
                    wmain[...],
                    operand(
                        lambda v, t=t: jnp.concatenate(
                            [it_v[v, k0 + j, rows(x, t), :] for j in range(2)], axis=1
                        )
                    ),
                    preferred_element_type=F32,
                )
                for t in range(2)
            ]

            def part(t, f, u, j):
                at = (u * 6 + f) * 8
                return y[t][at : at + 8, j * NR : (j + 1) * NR]

            w = [[fw_v[f, rows(x, t), :] for f in range(6)] for t in range(2)]
            w[0][2] = jnp.where(sub == 0, 0.0, w[0][2])
            w[1][3] = jnp.where(sub == 7, 0.0, w[1][3])
            for t in range(2):
                w[t][4] = jnp.where(lane == 0, 0.0, w[t][4])
                w[t][5] = jnp.where(lane == NR - 1, 0.0, w[t][5])
            left = [[[None] * V for _ in range(2)] for _ in range(2)]
            kept = [[[None] * V for _ in range(2)] for _ in range(2)]
            for u in range(V):
                for t in range(2):
                    for j in range(2):
                        y2, y3 = part(t, 2, u, j), part(t, 3, u, j)
                        if t == 1:
                            y2 = jnp.where(sub == 0, part(0, 2, u, j), y2)
                        else:
                            y3 = jnp.where(sub == 7, part(1, 3, u, j), y3)
                        total = w[t][2] * y2 + w[t][3] * y3
                        total += w[t][4] * pltpu.roll(part(t, 4, u, j), 1, axis=1)
                        total += w[t][5] * pltpu.roll(part(t, 5, u, j), NR - 1, axis=1)
                        if x > 0:
                            total += w[t][0] * before[t][j][u]
                            left_before[t][j][u] = left_before[t][j][u] - fw_v[1, rows(x - 1, t), :] * part(t, 1, u, j)
                        left[t][j][u] = rhs_v[u, k0 + j, rows(x, t), :] - total
                        kept[t][j][u] = part(t, 0, u, j)
            if x > 0:
                finish(x - 1, left_before)
            before, left_before = kept, left
        finish(CX - 1, left_before)

    def rest(first, last):
        @pl.loop(first, last)
        def _(i):
            k0, x = 2 * (i // CX), i % CX
            for t in range(2):
                at = pl.ds(pl.multiple_of(x * CG + 8 * t, 8), 8)
                rem = [[rhs_v[v, k0 + j, at, :] for v in range(V)] for j in range(2)]
                for u in range(1, V):
                    acc = [None, None]
                    for v in range(V):
                        b = binv_v[u, v, at, :]
                        for j in range(2):
                            term = b * rem[j][v]
                            acc[j] = term if acc[j] is None else acc[j] + term
                    for j in range(2):
                        upd[u, k0 + j, at, :] = acc[j]

    r = lax.broadcasted_iota(jnp.int32, (2 * NR, SLOTS), 0)
    lanes = (cell[...] % NR == r % NR).astype(BF16)
    r = lax.broadcasted_iota(jnp.int32, (ROWS, SLOTS), 0)
    on_row = (cell[...] // NR == r).astype(F32)

    @pl.loop(0, PAIRS)
    def _(c):
        rhs_copy(c).wait()
        for side in range(4):

            @pl.when(present[side])
            def _():
                halo_copy(side, c, side).wait_recv()

        for level, when in enumerate(HEARD):

            @pl.when(c == when)
            def _():
                relay_wait(level)
                relay_signal(level + 1)

        borders(c)
        main(c)
        for j in range(2):
            hi, lo = split(upd[0, 2 * c + j])
            both = jnp.concatenate([hi, lo], axis=1).astype(BF16)
            found = jnp.dot(both, lanes, preferred_element_type=F32) * on_row
            pick[pl.ds(2 * c + j, 1), :] = jnp.sum(found, axis=0, keepdims=True)

    pressure = pick[...]
    shapes = shape[...]
    values = jnp.concatenate(
        [pressure, shapes, jnp.broadcast_to(patch[...].astype(F32), (8, SLOTS))], axis=0
    )
    spread = jnp.concatenate([values] * 4, axis=0)
    group = lax.broadcasted_iota(jnp.int32, (NR, SLOTS), 0) // 32
    chosen = names.astype(BF16)
    chosen = jnp.concatenate([chosen, chosen], axis=1)
    for half in range(2):
        hi, lo = split(jnp.where(place == 4 * half + group, spread, 0.0))
        payload[:, half, :] = nt(chosen, jnp.concatenate([hi, lo], axis=1).astype(BF16))
    products = jnp.concatenate([shapes[m : m + 1] * pressure for m in range(8)], axis=0)
    sums = nt(jnp.ones((8, SLOTS), F32), products, HIGH)
    payload[:, 2, :] = jnp.broadcast_to(sums[0:1], (DEV, NR))

    relay_wait(len(ROUNDS) - 1)
    for step in STEPS:
        wall_copy(step).start()
    arrived[me] = payload[me]
    rest(0, PAIRS * CX)
    wall_all.wait_recv()
    arrived_out[...] = arrived[...]

    for c in range(PAIRS):
        for side in range(4):

            @pl.when(present[side])
            def _():
                halo_copy(side, c).wait_send()

    wall_all.wait_send()


def force_kernel(upd, arrived, upd_out, patch_out, force_out, patch_force, force, sem):
    copies = [
        pltpu.make_async_copy(upd.at[v], upd_out.at[v], sem.at[v]) for v in range(V)
    ]
    for copy in copies:
        copy.start()

    lane = lax.broadcasted_iota(jnp.int32, (2 * NR, NR), 0) % NR
    column = lax.broadcasted_iota(jnp.int32, (2 * NR, NR), 1)
    patch = lax.broadcasted_iota(jnp.int32, (DEV, NR), 1).astype(F32)
    total = None
    for half in range(2):
        hi, lo = split(arrived[:, half, :])
        both = jnp.concatenate([hi, lo], axis=1).astype(BF16)
        for j in range(4):
            base = 32 * j
            by_shape = (lane == base + K + column // K).astype(BF16)
            by_rhs = (lane == base + column % K).astype(BF16)
            by_patch = (lane == base + 24).astype(BF16)
            contribution = jnp.dot(both, by_shape, preferred_element_type=F32) * jnp.dot(
                both, by_rhs, preferred_element_type=F32
            )
            label = jnp.dot(both, by_patch, preferred_element_type=F32)
            member = (label == patch).astype(F32).T[0:PATCH_DEV].astype(BF16)
            hi, lo = split(contribution)
            term = jnp.dot(member, hi.astype(BF16), preferred_element_type=F32) + jnp.dot(
                member, lo.astype(BF16), preferred_element_type=F32
            )
            total = term if total is None else total + term
    patch_force[...] = total
    out_patch = pltpu.make_async_copy(patch_force, patch_out, sem.at[V])
    out_patch.start()
    sums = jnp.sum(arrived[:, 2, :], axis=0, keepdims=True) / jnp.sqrt(F32(DEV * SLOTS))
    r = lax.broadcasted_iota(jnp.int32, (8, NR), 0)
    c = lax.broadcasted_iota(jnp.int32, (8, NR), 1)
    rows = jnp.where(c // K == r, sums, 0.0)
    r = lax.broadcasted_iota(jnp.int32, (K, NR), 0)
    c = lax.broadcasted_iota(jnp.int32, (K, NR), 1)
    force[...] = nt(rows, (c % K == r).astype(F32), HIGH)
    out_force = pltpu.make_async_copy(force, force_out, sem.at[V + 1])
    out_force.start()
    for copy in copies:
        copy.wait()
    out_patch.wait()
    out_force.wait()


def shards(iterate, right_side, block_inverse, face_weight, face_jacobian, wall_cell, wall_owner, wall_patch, wall_shape):
    hbm = pl.BlockSpec(memory_space=pltpu.HBM)
    vmem = pl.BlockSpec(memory_space=pltpu.VMEM)
    dma = pltpu.SemaphoreType.DMA
    operands = (
        iterate.reshape(V, K, ROWS, NR),
        right_side.reshape(V, K, ROWS, NR),
        block_inverse.reshape(V, V, ROWS, NR),
        face_weight.reshape(6, ROWS, NR),
        face_jacobian,
        wall_cell.reshape(1, SLOTS),
        wall_owner.reshape(1, SLOTS),
        wall_patch.reshape(1, SLOTS),
        wall_shape.T,
    )
    updated, arrived = pl.pallas_call(
        sweep_kernel,
        out_shape=(
            pltpu.VMEM((V, K, ROWS, NR), F32),
            pltpu.VMEM((DEV, 3, NR), F32),
        ),
        in_specs=[hbm] * 9,
        out_specs=(vmem, vmem),
        scratch_shapes=[
            pltpu.VMEM((V, K, ROWS, NR), F32),
            pltpu.VMEM((V, K, ROWS, NR), F32),
            pltpu.VMEM((V, V, ROWS, NR), F32),
            pltpu.VMEM((6, ROWS, NR), F32),
            pltpu.VMEM((2, V, K, CG, NR), F32),
            pltpu.VMEM((2, V, K, CX, NR), F32),
            pltpu.VMEM((2, V, K, CX, NR), F32),
            pltpu.VMEM((6 * BLK, DEPTH), BF16),
            pltpu.VMEM((4, TERM, DEPTH), BF16),
            pltpu.VMEM((K, SLOTS), F32),
            pltpu.VMEM((6, V, V), F32),
            pltpu.VMEM((1, SLOTS), jnp.int32),
            pltpu.VMEM((1, SLOTS), jnp.int32),
            pltpu.VMEM((1, SLOTS), jnp.int32),
            pltpu.VMEM((8, SLOTS), F32),
            pltpu.VMEM((DEV, 3, NR), F32),
            pltpu.VMEM((DEV, 3, NR), F32),
            dma((PAIRS,)),
            dma((PAIRS,)),
            dma((7,)),
            dma((4, PAIRS)),
            dma((4, PAIRS)),
            dma,
            dma,
            pltpu.SemaphoreType.REGULAR((3, 6)),
        ],
        compiler_params=pltpu.CompilerParams(
            collective_id=0, has_side_effects=True, vmem_limit_bytes=32 * 1024 * 1024
        ),
    )(*[pltpu.with_memory_space_constraint(x, pltpu.HBM) for x in operands])
    updated, patch_force, force = pl.pallas_call(
        force_kernel,
        out_shape=(
            pltpu.HBM((V, K, ROWS, NR), F32),
            pltpu.HBM((PATCH_DEV, NR), F32),
            pltpu.HBM((8, K), F32),
        ),
        in_specs=[vmem, vmem],
        out_specs=(hbm, hbm, hbm),
        scratch_shapes=[
            pltpu.VMEM((PATCH_DEV, NR), F32),
            pltpu.VMEM((8, K), F32),
            dma((V + 2,)),
        ],
        compiler_params=pltpu.CompilerParams(vmem_limit_bytes=8 * 1024 * 1024),
    )(
        pltpu.with_memory_space_constraint(updated, pltpu.VMEM),
        pltpu.with_memory_space_constraint(arrived, pltpu.VMEM),
    )
    return (updated.reshape(V, K, CX, CG, NR), patch_force, force)


def solution(mesh):
    placed = (
        P(None, None, "stream", "girth", None),
        P(None, None, "stream", "girth", None),
        P(None, None, "stream", "girth", None),
        P(None, "stream", "girth", None),
        P(),
        P(("stream", "girth")),
        P(("stream", "girth"), None),
        P(("stream", "girth")),
        P(("stream", "girth"), None),
    )
    return jax.shard_map(
        shards,
        mesh=mesh,
        in_specs=placed,
        out_specs=(P(None, None, "stream", "girth", None), P(("stream", "girth"), None), P()),
        check_vma=False,
    )
```

```python
import jax
import jax.numpy as jnp
from jax import lax
from jax.experimental import pallas as pl
from jax.experimental.pallas import tpu as pltpu
from jax.sharding import PartitionSpec as P

V = 7
K = 16
CX = 8
CG = 16
NR = 128
ROWS = CX * CG
SLOTS = 256
PATCH_DEV = 32
NS = 8
NG = 16
DEV = NS * NG
PAIRS = K // 2
HEARD = (1, 4)
BLK = V * 8
TERM = 64
DEPTH = 3 * TERM
MESH = pl.DeviceIdType.MESH
HIGH = lax.Precision.HIGHEST
F32 = jnp.float32
BF16 = jnp.bfloat16
WEST, EAST, SOUTH, NORTH = range(4)
STEPS = sorted(
    [(a, b, c, d) for a in range(4) for b in range(2) for c in range(4) for d in range(4)][1:],
    key=lambda o: -sum(min(n, 4 - n) for n in (o[0], o[2], o[3])),
)
NEAR = [(0, 1, 0, 0)] + [
    (n if a == 0 else 0, b, n if a == 1 else 0, n if a == 2 else 0)
    for a in range(3) for n in (1, 3) for b in range(2)
]
ROUNDS = (
    tuple(o for o in NEAR if o[1] == 0),
    tuple((n, 0, 0, 0) for n in (1, 2, 3)),
    tuple((0, 0, n, 0) for n in (1, 2, 3)),
)


def nt(a, b, precision=None):
    return lax.dot_general(
        a, b, (((1,), (1,)), ((), ())), precision=precision, preferred_element_type=F32
    )


def split(x):
    hi = x.astype(BF16).astype(F32)
    return hi, x - hi


def operator(jacobian, turn):
    r = lax.broadcasted_iota(jnp.int32, (BLK, V), 0)
    c = lax.broadcasted_iota(jnp.int32, (BLK, V), 1)
    rows = (r // 8 == c).astype(F32)
    r = lax.broadcasted_iota(jnp.int32, (V, DEPTH), 0)
    c = lax.broadcasted_iota(jnp.int32, (V, DEPTH), 1)
    columns = ((c % TERM) // 8 == r).astype(F32)
    spread = jnp.dot(jnp.dot(rows, jacobian, precision=HIGH), columns, precision=HIGH)
    hi, lo = split(spread)
    r = lax.broadcasted_iota(jnp.int32, (BLK, DEPTH), 0)
    c = lax.broadcasted_iota(jnp.int32, (BLK, DEPTH), 1)
    keep = (r + turn) % 8 == c % 8
    return jnp.where(keep, jnp.where(c < 2 * TERM, hi, lo), 0.0)


def operand(load):
    pad = jnp.zeros((TERM - BLK, 2 * NR), F32)
    x = jnp.concatenate([load(v) for v in range(V)] + [pad], axis=0)
    hi = x.astype(BF16)
    lo = (x - hi.astype(F32)).astype(BF16)
    return jnp.concatenate([hi, lo, hi], axis=0)


def sweep_kernel(
    it, rhs, binv, fw, jac_in, cell_in, owner_in, patch_in, shape_in,
    upd, arrived_out,
    it_v, rhs_v, binv_v, fw_v, halo_x, halo_g, send_g, wmain, wside, pick,
    jac, cell, owner, patch, shape, payload, arrived,
    sem_it, sem_rhs, sem_misc, send_sem, recv_sem, out_sem, in_sem, relay,
):
    s, g = lax.axis_index("stream"), lax.axis_index("girth")
    present = (s > 0, s < NS - 1, g > 0, g < NG - 1)
    target = ((s - 1, g), (s + 1, g), (s, g - 1), (s, g + 1))

    def it_copy(c):
        ks = pl.ds(2 * c, 2)
        return pltpu.make_async_copy(it.at[:, ks], it_v.at[:, ks], sem_it.at[c])

    def rhs_copy(c):
        ks = pl.ds(2 * c, 2)
        return pltpu.make_async_copy(rhs.at[:, ks], rhs_v.at[:, ks], sem_rhs.at[c])

    singles = [
        pltpu.make_async_copy(a, b, sem_misc.at[i])
        for i, (a, b) in enumerate(
            (
                (jac_in, jac),
                (cell_in, cell),
                (owner_in, owner),
                (patch_in, patch),
                (shape_in, shape),
                (fw, fw_v),
                (binv, binv_v),
            )
        )
    ]

    def halo_copy(side, c, land=None):
        land = side ^ 1 if land is None else land
        ks = pl.ds(2 * c, 2)
        if side in (WEST, EAST):
            rows = pl.ds(0 if side == WEST else ROWS - CG, CG)
            src, dst = it_v.at[:, ks, rows], halo_x.at[land, :, ks]
        else:
            src, dst = send_g.at[side - 2, :, ks], halo_g.at[land - 2, :, ks]
        return pltpu.make_async_remote_copy(
            src_ref=src,
            dst_ref=dst,
            send_sem=send_sem.at[side, c],
            recv_sem=recv_sem.at[land, c],
            device_id=target[side],
            device_id_type=MESH,
        )

    me = s * NG + g
    y, core, z, x4 = s // 2, lax.rem(s, 2), g // 4, lax.rem(g, 4)
    by_y = [2 * lax.rem(y + n, 4) for n in range(4)]
    by_core = [lax.rem(core + n, 2) for n in range(2)]
    by_z = [4 * lax.rem(z + n, 4) for n in range(4)]
    by_x = [lax.rem(x4 + n, 4) for n in range(4)]

    def at(step):
        return (by_y[step[0]] + by_core[step[1]], by_z[step[2]] + by_x[step[3]])

    def wall_copy(step):
        to = at(step)
        return pltpu.make_async_remote_copy(
            src_ref=payload.at[to[0] * NG + to[1]],
            dst_ref=arrived.at[me],
            send_sem=out_sem,
            recv_sem=in_sem,
            device_id=to,
            device_id_type=MESH,
        )

    others = pl.ds(0, DEV - 1)
    wall_all = pltpu.make_async_remote_copy(
        src_ref=payload.at[others],
        dst_ref=arrived.at[others],
        send_sem=out_sem,
        recv_sem=in_sem,
        device_id=(by_y[0] + by_core[1], g),
        device_id_type=MESH,
    )

    def relay_signal(level):
        for i, step in enumerate(ROUNDS[level]):
            pl.semaphore_signal(relay.at[level, i], inc=1, device_id=at(step), device_id_type=MESH)

    def relay_wait(level):
        for i in range(len(ROUNDS[level])):
            pl.semaphore_wait(relay.at[level, i], 1)

    def send(c):
        it_copy(c).wait()
        for k in (2 * c, 2 * c + 1):
            for v in range(V):
                send_g[0, v, k] = it_v[v, k, pl.ds(0, CX, stride=CG), :]
                send_g[1, v, k] = it_v[v, k, pl.ds(CG - 1, CX, stride=CG), :]
        for side in range(4):

            @pl.when(present[side])
            def _():
                halo_copy(side, c).start()

    for c in range(2):
        it_copy(c).start()

    barrier = pltpu.get_barrier_semaphore()
    for to in [at(step) for step in NEAR] + [(s, lax.rem(g + 1, NG)), (s, lax.rem(g + NG - 1, NG))]:
        pl.semaphore_signal(barrier, inc=1, device_id=to, device_id_type=MESH)

    for copy in singles:
        copy.start()
    rhs_copy(0).start()

    pl.semaphore_wait(barrier, len(NEAR) + 2)
    for c in range(2):
        send(c)
    for c in range(2, PAIRS):
        it_copy(c).start()
    for c in range(1, PAIRS):
        rhs_copy(c).start()
    relay_signal(0)

    for side in range(4):

        @pl.when(jnp.logical_not(present[side]))
        def _():
            if side in (WEST, EAST):
                halo_x[side] = jnp.zeros((V, K, CG, NR), F32)
            else:
                halo_g[side - 2] = jnp.zeros((V, K, CX, NR), F32)

    for copy in singles[:5]:
        copy.wait()

    turns = (0, 0, 7, 1, 0, 0)
    parts = [operator(jac[f], turns[f]) for f in range(6)]
    wmain[...] = jnp.concatenate(
        [parts[f][8 * u : 8 * u + 8] for u in range(V) for f in range(6)], axis=0
    ).astype(BF16)
    pad = jnp.zeros((TERM - BLK, DEPTH), F32)
    for f in range(4):
        wside[f] = jnp.concatenate([operator(jac[f], 0), pad], axis=0).astype(BF16)

    names = (owner[...] == lax.broadcasted_iota(jnp.int32, (DEV, SLOTS), 0)).astype(F32)
    r = lax.broadcasted_iota(jnp.int32, (SLOTS, SLOTS), 0)
    c = lax.broadcasted_iota(jnp.int32, (SLOTS, SLOTS), 1)
    earlier = jnp.dot(names.astype(BF16), (r < c).astype(BF16), preferred_element_type=F32)
    place = jnp.sum(names * earlier, axis=0, keepdims=True).astype(jnp.int32)

    for copy in singles[5:]:
        copy.wait()

    sub = lax.broadcasted_iota(jnp.int32, (8, NR), 0)
    lane = lax.broadcasted_iota(jnp.int32, (8, NR), 1)

    def rows(x, t):
        return pl.ds(x * CG + 8 * t, 8)

    def borders(c):
        k0 = 2 * c
        for side in range(4):
            for t in range(2 if side in (WEST, EAST) else 1):
                if side in (WEST, EAST):
                    where = rows(0 if side == WEST else CX - 1, t)

                    def load(v):
                        return jnp.concatenate(
                            [halo_x[side, v, k0 + j, pl.ds(8 * t, 8), :] for j in range(2)], axis=1
                        )
                else:
                    where = pl.ds(0 if side == SOUTH else CG - 1, CX, stride=CG)

                    def load(v):
                        return jnp.concatenate([halo_g[side - 2, v, k0 + j] for j in range(2)], axis=1)

                z = jnp.dot(wside[side], operand(load), preferred_element_type=F32)
                w = fw_v[side, where, :]
                for j in range(2):
                    change = None
                    for u in range(V):
                        image = w * z[u * 8 : u * 8 + 8, j * NR : (j + 1) * NR]
                        rhs_v[u, k0 + j, where, :] = rhs_v[u, k0 + j, where, :] - image
                        term = binv_v[0, u, where, :] * image
                        change = term if change is None else change + term
                    upd[0, k0 + j, where, :] = upd[0, k0 + j, where, :] - change

    def main(c):
        k0 = 2 * c

        def finish(x, left):
            for t in range(2):
                for j in range(2):
                    acc = None
                    for v in range(V):
                        rhs_v[v, k0 + j, rows(x, t), :] = left[t][j][v]
                        term = binv_v[0, v, rows(x, t), :] * left[t][j][v]
                        acc = term if acc is None else acc + term
                    upd[0, k0 + j, rows(x, t), :] = acc

        before, left_before = None, None
        for x in range(CX):
            y = [
                jnp.dot(
                    wmain[...],
                    operand(
                        lambda v, t=t: jnp.concatenate(
                            [it_v[v, k0 + j, rows(x, t), :] for j in range(2)], axis=1
                        )
                    ),
                    preferred_element_type=F32,
                )
                for t in range(2)
            ]

            def part(t, f, u, j):
                at = (u * 6 + f) * 8
                return y[t][at : at + 8, j * NR : (j + 1) * NR]

            w = [[fw_v[f, rows(x, t), :] for f in range(6)] for t in range(2)]
            w[0][2] = jnp.where(sub == 0, 0.0, w[0][2])
            w[1][3] = jnp.where(sub == 7, 0.0, w[1][3])
            for t in range(2):
                w[t][4] = jnp.where(lane == 0, 0.0, w[t][4])
                w[t][5] = jnp.where(lane == NR - 1, 0.0, w[t][5])
            left = [[[None] * V for _ in range(2)] for _ in range(2)]
            kept = [[[None] * V for _ in range(2)] for _ in range(2)]
            for u in range(V):
                for t in range(2):
                    for j in range(2):
                        y2, y3 = part(t, 2, u, j), part(t, 3, u, j)
                        if t == 1:
                            y2 = jnp.where(sub == 0, part(0, 2, u, j), y2)
                        else:
                            y3 = jnp.where(sub == 7, part(1, 3, u, j), y3)
                        total = w[t][2] * y2 + w[t][3] * y3
                        total += w[t][4] * pltpu.roll(part(t, 4, u, j), 1, axis=1)
                        total += w[t][5] * pltpu.roll(part(t, 5, u, j), NR - 1, axis=1)
                        if x > 0:
                            total += w[t][0] * before[t][j][u]
                            left_before[t][j][u] = left_before[t][j][u] - fw_v[1, rows(x - 1, t), :] * part(t, 1, u, j)
                        left[t][j][u] = rhs_v[u, k0 + j, rows(x, t), :] - total
                        kept[t][j][u] = part(t, 0, u, j)
            if x > 0:
                finish(x - 1, left_before)
            before, left_before = kept, left
        finish(CX - 1, left_before)

    def rest(first, last):
        @pl.loop(first, last)
        def _(i):
            k0, x = 2 * (i // CX), i % CX
            for t in range(2):
                at = pl.ds(pl.multiple_of(x * CG + 8 * t, 8), 8)
                rem = [[rhs_v[v, k0 + j, at, :] for v in range(V)] for j in range(2)]
                for u in range(1, V):
                    acc = [None, None]
                    for v in range(V):
                        b = binv_v[u, v, at, :]
                        for j in range(2):
                            term = b * rem[j][v]
                            acc[j] = term if acc[j] is None else acc[j] + term
                    for j in range(2):
                        upd[u, k0 + j, at, :] = acc[j]

    r = lax.broadcasted_iota(jnp.int32, (2 * NR, SLOTS), 0)
    lanes = (cell[...] % NR == r % NR).astype(BF16)
    r = lax.broadcasted_iota(jnp.int32, (ROWS, SLOTS), 0)
    on_row = (cell[...] // NR == r).astype(F32)

    @pl.loop(0, PAIRS + 1)
    def _(i):
        for level, when in enumerate(HEARD):

            @pl.when(i == when)
            def _():
                relay_wait(level)
                relay_signal(level + 1)

        @pl.when(i < PAIRS // 2 - 1)
        def _():
            send(2 * i + 2)
            send(2 * i + 3)

        @pl.when(i < PAIRS)
        def _():
            rhs_copy(i).wait()
            main(i)

        @pl.when(i > 0)
        def _():
            c = i - 1
            for side in range(4):

                @pl.when(present[side])
                def _():
                    halo_copy(side, c, side).wait_recv()

            borders(c)
            for j in range(2):
                hi, lo = split(upd[0, 2 * c + j])
                both = jnp.concatenate([hi, lo], axis=1).astype(BF16)
                found = jnp.dot(both, lanes, preferred_element_type=F32) * on_row
                pick[pl.ds(2 * c + j, 1), :] = jnp.sum(found, axis=0, keepdims=True)

    pressure = pick[...]
    shapes = shape[...]
    values = jnp.concatenate(
        [pressure, shapes, jnp.broadcast_to(patch[...].astype(F32), (8, SLOTS))], axis=0
    )
    spread = jnp.concatenate([values] * 4, axis=0)
    group = lax.broadcasted_iota(jnp.int32, (NR, SLOTS), 0) // 32
    chosen = names.astype(BF16)
    chosen = jnp.concatenate([chosen, chosen], axis=1)
    for half in range(2):
        hi, lo = split(jnp.where(place == 4 * half + group, spread, 0.0))
        payload[:, half, :] = nt(chosen, jnp.concatenate([hi, lo], axis=1).astype(BF16))
    products = jnp.concatenate([shapes[m : m + 1] * pressure for m in range(8)], axis=0)
    sums = nt(jnp.ones((8, SLOTS), F32), products, HIGH)
    payload[:, 2, :] = jnp.broadcast_to(sums[0:1], (DEV, NR))

    relay_wait(len(ROUNDS) - 1)
    for step in STEPS:
        wall_copy(step).start()
    arrived[me] = payload[me]
    rest(0, PAIRS * CX)
    for c in range(PAIRS):
        for side in range(4):

            @pl.when(present[side])
            def _():
                halo_copy(side, c).wait_send()

    wall_all.wait_recv()
    arrived_out[...] = arrived[...]

    wall_all.wait_send()


def force_kernel(upd, arrived, upd_out, patch_out, force_out, patch_force, force, sem):
    out_field = pltpu.make_async_copy(upd, upd_out, sem.at[2])
    out_field.start()

    lane = lax.broadcasted_iota(jnp.int32, (2 * NR, NR), 0) % NR
    column = lax.broadcasted_iota(jnp.int32, (2 * NR, NR), 1)
    patch = lax.broadcasted_iota(jnp.int32, (DEV, NR), 1).astype(F32)
    total = None
    for half in range(2):
        hi, lo = split(arrived[:, half, :])
        both = jnp.concatenate([hi, lo], axis=1).astype(BF16)
        for j in range(4):
            base = 32 * j
            by_shape = (lane == base + K + column // K).astype(BF16)
            by_rhs = (lane == base + column % K).astype(BF16)
            by_patch = (lane == base + 24).astype(BF16)
            contribution = jnp.dot(both, by_shape, preferred_element_type=F32) * jnp.dot(
                both, by_rhs, preferred_element_type=F32
            )
            label = jnp.dot(both, by_patch, preferred_element_type=F32)
            member = (label == patch).astype(F32).T[0:PATCH_DEV].astype(BF16)
            hi, lo = split(contribution)
            term = jnp.dot(member, hi.astype(BF16), preferred_element_type=F32) + jnp.dot(
                member, lo.astype(BF16), preferred_element_type=F32
            )
            total = term if total is None else total + term
    patch_force[...] = total
    out_patch = pltpu.make_async_copy(patch_force, patch_out, sem.at[0])
    out_patch.start()
    sums = jnp.sum(arrived[:, 2, :], axis=0, keepdims=True) / jnp.sqrt(F32(DEV * SLOTS))
    r = lax.broadcasted_iota(jnp.int32, (8, NR), 0)
    c = lax.broadcasted_iota(jnp.int32, (8, NR), 1)
    rows = jnp.where(c // K == r, sums, 0.0)
    r = lax.broadcasted_iota(jnp.int32, (K, NR), 0)
    c = lax.broadcasted_iota(jnp.int32, (K, NR), 1)
    force[...] = nt(rows, (c % K == r).astype(F32), HIGH)
    out_force = pltpu.make_async_copy(force, force_out, sem.at[1])
    out_force.start()
    out_field.wait()
    out_patch.wait()
    out_force.wait()


def shards(iterate, right_side, block_inverse, face_weight, face_jacobian, wall_cell, wall_owner, wall_patch, wall_shape):
    hbm = pl.BlockSpec(memory_space=pltpu.HBM)
    vmem = pl.BlockSpec(memory_space=pltpu.VMEM)
    dma = pltpu.SemaphoreType.DMA
    operands = (
        iterate.reshape(V, K, ROWS, NR),
        right_side.reshape(V, K, ROWS, NR),
        block_inverse.reshape(V, V, ROWS, NR),
        face_weight.reshape(6, ROWS, NR),
        face_jacobian,
        wall_cell.reshape(1, SLOTS),
        wall_owner.reshape(1, SLOTS),
        wall_patch.reshape(1, SLOTS),
        wall_shape.T,
    )
    updated, arrived = pl.pallas_call(
        sweep_kernel,
        out_shape=(
            pltpu.VMEM((V, K, ROWS, NR), F32),
            pltpu.VMEM((DEV, 3, NR), F32),
        ),
        in_specs=[hbm] * 9,
        out_specs=(vmem, vmem),
        scratch_shapes=[
            pltpu.VMEM((V, K, ROWS, NR), F32),
            pltpu.VMEM((V, K, ROWS, NR), F32),
            pltpu.VMEM((V, V, ROWS, NR), F32),
            pltpu.VMEM((6, ROWS, NR), F32),
            pltpu.VMEM((2, V, K, CG, NR), F32),
            pltpu.VMEM((2, V, K, CX, NR), F32),
            pltpu.VMEM((2, V, K, CX, NR), F32),
            pltpu.VMEM((6 * BLK, DEPTH), BF16),
            pltpu.VMEM((4, TERM, DEPTH), BF16),
            pltpu.VMEM((K, SLOTS), F32),
            pltpu.VMEM((6, V, V), F32),
            pltpu.VMEM((1, SLOTS), jnp.int32),
            pltpu.VMEM((1, SLOTS), jnp.int32),
            pltpu.VMEM((1, SLOTS), jnp.int32),
            pltpu.VMEM((8, SLOTS), F32),
            pltpu.VMEM((DEV, 3, NR), F32),
            pltpu.VMEM((DEV, 3, NR), F32),
            dma((PAIRS,)),
            dma((PAIRS,)),
            dma((7,)),
            dma((4, PAIRS)),
            dma((4, PAIRS)),
            dma,
            dma,
            pltpu.SemaphoreType.REGULAR((3, 6)),
        ],
        compiler_params=pltpu.CompilerParams(
            collective_id=0, has_side_effects=True, vmem_limit_bytes=32 * 1024 * 1024
        ),
    )(*[pltpu.with_memory_space_constraint(x, pltpu.HBM) for x in operands])
    updated, patch_force, force = pl.pallas_call(
        force_kernel,
        out_shape=(
            pltpu.HBM((V, K, ROWS, NR), F32),
            pltpu.HBM((PATCH_DEV, NR), F32),
            pltpu.HBM((8, K), F32),
        ),
        in_specs=[vmem, vmem],
        out_specs=(hbm, hbm, hbm),
        scratch_shapes=[
            pltpu.VMEM((PATCH_DEV, NR), F32),
            pltpu.VMEM((8, K), F32),
            dma((3,)),
        ],
        compiler_params=pltpu.CompilerParams(vmem_limit_bytes=8 * 1024 * 1024),
    )(
        pltpu.with_memory_space_constraint(updated, pltpu.VMEM),
        pltpu.with_memory_space_constraint(arrived, pltpu.VMEM),
    )
    return (updated.reshape(V, K, CX, CG, NR), patch_force, force)


def solution(mesh):
    placed = (
        P(None, None, "stream", "girth", None),
        P(None, None, "stream", "girth", None),
        P(None, None, "stream", "girth", None),
        P(None, "stream", "girth", None),
        P(),
        P(("stream", "girth")),
        P(("stream", "girth"), None),
        P(("stream", "girth")),
        P(("stream", "girth"), None),
    )
    return jax.shard_map(
        shards,
        mesh=mesh,
        in_specs=placed,
        out_specs=(P(None, None, "stream", "girth", None), P(("stream", "girth"), None), P()),
        check_vma=False,
    )
```
